32 devices in a mesh: pair: 8 (over z, core), virt: 4 (over y, x).
Axes of the slice: x: 2, y: 2, z: 4, core: 2. Of those that a mesh axis runs over, the one named last changes fastest.
Arguments:
- amplitudes: float32 [16, 1024, 4096], P('virt', 'pair'), may hold values from -0.9 to 0.9
- integrals: float32 [16, 384, 4096], P('virt', 'pair'), may hold values from -0.09375 to 0.09375
- tile_flags: int32 [16], P('virt'), may hold values 0 or 1
- live_count: int32 [4], replicated, may hold values from 1 to 4, as said below
- pair_occ: int32 [1024, 2], P(('pair', 'virt')), may hold values from 0 to 199
- occ_energy: float32 [200], replicated, may hold values from -2.5 to -0.3
- ab_energy: float32 [384], replicated, may hold values from 0.6 to 3
Outputs:
- ladder: float32 [1024, 384], P(('pair', 'virt'))
- update: float32 [1024, 384], P(('pair', 'virt'))
The draws below stay inside these ranges and needn't reach their ends.
Inputs may be any that keep to these rules, and one draw needn't show every extreme that they name: `live_count`: entry v is how many of the 4 slots of virt index v hold tile pairs: its slots below that number do, and the contents of the others are not to be used. At some index it is 4, and at the index half the axis away it is 1.
All inputs are finite; a program needn't handle non-finite values. No bound on the sum of `tile_flags` on one device may be relied on, other than what follows from the above.
Results may differ from the reference program's by a relative error of at most 0.0001.
Values sent between devices are 32-bit elements; how exact they have to be, the bound alone decides.
A program may use at most 128 MiB of HBM per device.

```python
import jax
import jax.numpy as jnp
from jax import lax

TILE = 64
NOCC = 200
SLOTS = 4
AB = 384
TT = 4096
PAIRS = 1024
TILES = 16
N_VIRT = 4


def draw_live_count(key, part):
    key_one, key_two, key_three = jax.random.split(key, 3)
    first_draw = jax.random.randint(key_one, (N_VIRT,), 1, SLOTS + 1)
    second_draw = jax.random.randint(key_two, (N_VIRT,), 1, SLOTS + 1)
    counts = jnp.minimum(first_draw, second_draw)
    full_index = jax.random.randint(key_three, (), 0, N_VIRT)
    positions = jnp.arange(N_VIRT)
    counts = jnp.where(positions == full_index, SLOTS, counts)
    counts = jnp.where(positions == (full_index + N_VIRT // 2) % N_VIRT, 1, counts)
    return counts.astype(jnp.int32)


def touch_ends(values, rng, smallest, largest):
    place = [jax.random.randint(jax.random.fold_in(rng, axis), (), 0, length) for axis, length in enumerate(values.shape)]
    main_axis = values.shape.index(max(values.shape))
    beside = place[:main_axis] + [(place[main_axis] + 1) % values.shape[main_axis]] + place[main_axis + 1:]
    return values.at[tuple(place)].set(smallest).at[tuple(beside)].set(largest)


def spiked(entries, rng, source, target, parts, factor):
    owner, partner = [(jnp.arange(entries.shape[dim]) // (entries.shape[dim] // parts)).reshape([-1 if axis == dim else 1 for axis in range(entries.ndim)]) for dim in (source, target)]
    chosen = jax.random.permutation(rng, parts)[partner]
    strong = (owner == chosen) | (owner == (partner + parts // 2) % parts)
    return jnp.where(strong, factor * entries, entries)


def shard_levels(rng, extent, pieces, least, top_value):
    def one(axis_at, blocks):
        steps = jax.random.uniform(jax.random.fold_in(jax.random.fold_in(rng, 6), axis_at), (blocks,), jnp.float32, least / len(pieces), top_value / len(pieces))
        return jnp.repeat(jnp.exp(steps), extent[axis_at] // blocks).reshape((-1,) + (1,) * (len(extent) - axis_at - 1))

    loudness = one(*pieces[0])
    for cut in pieces[1:]:
        loudness = loudness * one(*cut)
    return loudness


def scatter_about(key, dims, deviation, limit, shards=(), kind=jnp.bfloat16):
    loudness = shard_levels(key, dims, shards, -0.22, 0.18) if shards else 1.0
    drawn = jax.random.normal(key, dims, jnp.float32) * deviation * loudness
    return jnp.minimum(jnp.maximum(drawn, -limit), limit).astype(kind)


def noise_with(own_key, shape, scale, bound, cuts, heavy, kind=jnp.bfloat16):
    entries = scale * jax.random.normal(own_key, shape, jnp.float32)
    if cuts:
        entries = entries * shard_levels(own_key, shape, cuts, -0.22, 0.18)
    return jnp.clip(spiked(entries, jax.random.fold_in(own_key, 3), *heavy), -bound, bound).astype(kind)


def setup_inputs(seed: int = 0) -> dict:
    key_list = jax.random.split(jax.random.key(seed), 8)
    amplitudes = noise_with(key_list[0], (TILES, PAIRS, TT), 0.15, 0.9, ((0, 4), (1, 8)), (0, 1, 8, 2.0), jnp.float32)
    integrals = scatter_about(key_list[1], (TILES, AB, TT), TT ** -0.5, 0.09375, ((0, 4), (1, 8)), jnp.float32)
    tile_flags = touch_ends((jax.random.randint(key_list[2], (TILES,), 0, 2) < 1).astype(jnp.int32), jax.random.fold_in(key_list[2], 1), 0, 1)
    live_count = draw_live_count(jax.random.fold_in(key_list[7], 71), 0)
    pair_occ = touch_ends(jax.random.randint(key_list[4], (PAIRS, 2), 0, NOCC), jax.random.fold_in(key_list[4], 1), 0, NOCC - 1).astype(jnp.int32)
    occ_energy = jnp.clip(jax.random.uniform(key_list[5], (NOCC,), jnp.float32, -2.5, -0.3), -2.5, -0.3)
    ab_energy = jnp.clip(jax.random.uniform(key_list[6], (AB,), jnp.float32, 0.6, 3.0), 0.6, 3.0)
    return {"amplitudes": amplitudes, "integrals": integrals, "tile_flags": tile_flags, "live_count": live_count, "pair_occ": pair_occ, "occ_energy": occ_energy, "ab_energy": ab_energy}


def symmetric(integrals, tile_flags):
    shaped = integrals.reshape(integrals.shape[0], integrals.shape[1], TILE, TILE)
    swapped = jnp.swapaxes(shaped, 2, 3).reshape(integrals.shape)
    return integrals + tile_flags.astype(jnp.float32)[:, None, None] * swapped


def reference(amplitudes, integrals, tile_flags, live_count, pair_occ, occ_energy, ab_energy):
    slot_index = jnp.arange(TILES, dtype=jnp.int32)
    live_mask = ((slot_index % SLOTS) < live_count[slot_index // SLOTS]).astype(jnp.float32)
    sym_integrals = symmetric(integrals, tile_flags)

    def one_tile(running, tile_items):
        amp_tile, int_tile, weight = tile_items
        tile_term = lax.dot_general(amp_tile, int_tile, (((1,), (1,)), ((), ())),
                                    precision=lax.Precision.HIGHEST,
                                    preferred_element_type=jnp.float32)
        return running + weight * tile_term, None

    ladder = lax.scan(one_tile, jnp.zeros((PAIRS, AB), jnp.float32),
                      (amplitudes, sym_integrals, live_mask))[0]
    first_energy = occ_energy[pair_occ[:, 0]]
    second_energy = occ_energy[pair_occ[:, 1]]
    denominator = ab_energy[None, :] - first_energy[:, None] - second_energy[:, None]
    return ladder, ladder / denominator
```

```python
import functools

import jax
import jax.numpy as jnp
from jax import lax
from jax.experimental import pallas as pl
from jax.experimental.pallas import tpu as pltpu
from jax.sharding import PartitionSpec as P

TILE = 64
CORES = 2
DEPTH = 512
MESH = pl.DeviceIdType.MESH


def symmetric(integrals, tile_flags):
    shaped = integrals.reshape(integrals.shape[0], integrals.shape[1], TILE, TILE)
    swapped = jnp.swapaxes(shaped, 2, 3).reshape(integrals.shape)
    return integrals + tile_flags.astype(jnp.float32)[:, None, None] * swapped


def split(x):
    high = x.astype(jnp.bfloat16)
    return high, (x - high.astype(jnp.float32)).astype(jnp.bfloat16)


def product(a, b):
    a_high, a_low = split(a)
    b_high, b_low = split(b)

    def dot(x, y):
        return lax.dot_general(x, y, (((1,), (1,)), ((), ())), preferred_element_type=jnp.float32)

    return dot(a_high, b_high) + (dot(a_high, b_low) + dot(a_low, b_high))


def kernel(queue, swaps, chips, n_virt, counts, a_ref, v_ref, out_ref, rows_all, a_out, a_in, v_out, v_in, acc, parts,
           xs, xr, zs, zr, cs, cr, rs, rr):
    pair = lax.axis_index("pair")
    virt = lax.axis_index("virt")
    z, core = pair // CORES, pair % CORES
    half = a_ref.shape[2] // 2
    slots = a_ref.shape[0]
    rows = v_ref.shape[1]
    pairs = a_ref.shape[1]
    out_rows = out_ref.shape[0]
    partner = lax.rem(virt + n_virt // 2, n_virt)
    live, keep, taken = counts[0], counts[1], counts[2]

    def chip_at(target):
        return (target * CORES + core, virt)

    twin = (z * CORES + 1 - core, virt)
    barrier = pltpu.get_barrier_semaphore()
    pl.semaphore_signal(barrier, inc=1, device_id=twin, device_id_type=MESH)
    for step in range(1, n_virt):
        pl.semaphore_signal(barrier, inc=1, device_id=(pair, lax.rem(virt + step, n_virt)), device_id_type=MESH)

    @pl.when(z > 0)
    def _():
        pl.semaphore_signal(barrier, inc=1, device_id=chip_at(z - 1), device_id_type=MESH)

    @pl.when(z < chips - 1)
    def _():
        pl.semaphore_signal(barrier, inc=1, device_id=chip_at(z + 1), device_id_type=MESH)

    greeted = n_virt + jnp.where(z > 0, 1, 0) + jnp.where(z < chips - 1, 1, 0)
    pl.semaphore_wait(barrier, greeted)

    def block(q, chip, core_at):
        start = pl.multiple_of((chip * CORES + core_at) * rows, 8)
        return rows_all.at[q, pl.ds(start, rows), :]

    def swap_a(j):
        return pltpu.make_async_remote_copy(
            src_ref=a_out.at[j], dst_ref=a_in.at[j], send_sem=xs.at[0, j], recv_sem=xr.at[0, j],
            device_id=(pair, partner), device_id_type=MESH)

    def swap_v(j):
        return pltpu.make_async_remote_copy(
            src_ref=v_out.at[j], dst_ref=v_in.at[j], send_sem=xs.at[1, j], recv_sem=xr.at[1, j],
            device_id=(pair, partner), device_id_type=MESH)

    def to_chip(q, way, hops):
        sign = 1 if way == 0 else -1
        ref = block(q, z - sign * hops, core)
        return pltpu.make_async_remote_copy(
            src_ref=ref, dst_ref=ref, send_sem=zs.at[q, way, hops], recv_sem=zr.at[q, way, hops],
            device_id=chip_at(z + sign), device_id_type=MESH)

    def from_chip(q, way, hops):
        sign = 1 if way == 0 else -1
        ref = block(q, z - sign * hops, core)
        return pltpu.make_async_remote_copy(
            src_ref=ref, dst_ref=ref, send_sem=zs.at[q, way, hops - 1], recv_sem=zr.at[q, way, hops - 1],
            device_id=chip_at(z - sign), device_id_type=MESH)

    def to_twin(q, chip):
        ref = block(q, chip, core)
        return pltpu.make_async_remote_copy(
            src_ref=ref, dst_ref=ref, send_sem=cs.at[q, chip], recv_sem=cr.at[q, chip],
            device_id=twin, device_id_type=MESH)

    def from_twin(q, chip):
        ref = block(q, chip, 1 - core)
        return pltpu.make_async_remote_copy(
            src_ref=ref, dst_ref=ref, send_sem=cs.at[q, chip], recv_sem=cr.at[q, chip],
            device_id=twin, device_id_type=MESH)

    def can_send(way, hops):
        if way == 0:
            return (z - hops >= 0) & (z < chips - 1)
        return (z + hops < chips) & (z > 0)

    def can_get(way, hops):
        return z - hops >= 0 if way == 0 else z + hops < chips

    def columns(unit):
        return slice((unit % 2) * half, (unit % 2 + 1) * half)

    for j in range(swaps):
        slot = jnp.clip(live + (j - swaps) // 2, 0, slots - 1)
        v_out[j] = v_ref[slot, :, columns(j - swaps)]
        swap_v(j).start()
    for j in range(swaps):
        slot = jnp.clip(live + (j - swaps) // 2, 0, slots - 1)
        a_out[j] = a_ref[slot, :, columns(j - swaps)]
        swap_a(j).start()

    def stage(q):
        own_unit = min(q, 2 * slots - 1)
        own = v_ref[own_unit // 2, :, columns(own_unit)]
        j = q - (queue - swaps)
        if j >= 0:
            swap_v(j).wait_recv()
            own = jnp.where(q >= queue - taken, v_in[j], own)
        start = pl.multiple_of(pair * rows, 8)
        rows_all[q, pl.ds(start, rows), :] = own
        for way in range(2):
            @pl.when(can_send(way, 0))
            def _():
                to_chip(q, way, 0).start()
        to_twin(q, z).start()

    def relay(q):
        for hops in range(1, chips):
            for way in range(2):
                @pl.when(can_get(way, hops))
                def _():
                    from_chip(q, way, hops).wait_recv()
                    if hops < chips - 1:
                        @pl.when(can_send(way, hops))
                        def _():
                            to_chip(q, way, hops).start()
                    to_twin(q, z - hops if way == 0 else z + hops).start()

    def multiply(q):
        for chip in range(chips):
            from_twin(q, chip).wait_recv()
        own_unit = min(q, 2 * slots - 1)
        j = q - (queue - swaps)
        if j >= 0:
            swap_a(j).wait_recv()
        keep_own = q < keep
        base = (own_unit % 2) * half

        @pl.loop(0, half // DEPTH)
        def _(step):
            inner = pl.ds(pl.multiple_of(step * DEPTH, DEPTH), DEPTH)
            outer = pl.ds(pl.multiple_of(base + step * DEPTH, DEPTH), DEPTH)
            a = jnp.where(keep_own, a_ref[own_unit // 2, :, outer], 0.0)
            if j >= 0:
                a = jnp.where(q >= queue - taken, a_in[j, :, inner], a)
            acc[...] += product(a, rows_all[q, :, inner])

    acc[...] = jnp.zeros_like(acc)
    ahead = queue - swaps
    for q in range(ahead):
        stage(q)
    for q in range(queue):
        relay(q)
        if q + ahead < queue:
            stage(q + ahead)
        multiply(q)

    def part(step):
        to = lax.rem(virt + step, n_virt)
        ref = acc.at[pl.ds(pl.multiple_of(to * out_rows, 8), out_rows), :]
        return pltpu.make_async_remote_copy(
            src_ref=ref, dst_ref=parts.at[step - 1], send_sem=rs.at[step - 1], recv_sem=rr.at[step - 1],
            device_id=(pair, to), device_id_type=MESH)

    for step in range(1, n_virt):
        part(step).start()
    total = acc[pl.ds(pl.multiple_of(virt * out_rows, 8), out_rows), :]
    for step in range(1, n_virt):
        part(step).wait_recv()
        total = total + parts[step - 1]
    out_ref[...] = total

    for step in range(1, n_virt):
        part(step).wait_send()
    for j in range(swaps):
        swap_a(j).wait_send()
        swap_v(j).wait_send()
    for q in range(queue):
        for hops in range(chips - 1):
            for way in range(2):
                @pl.when(can_send(way, hops))
                def _():
                    to_chip(q, way, hops).wait_send()
        for chip in range(chips):
            to_twin(q, chip).wait_send()


def contract(queue, call_id, chips, n_virt, counts, amplitudes, integrals):
    slots, pairs, width = amplitudes.shape
    rows = integrals.shape[1]
    ab = rows * chips * CORES
    swaps, half = slots - 1, width // 2
    f32 = jnp.float32
    dma = pltpu.SemaphoreType.DMA
    return pl.pallas_call(
        functools.partial(kernel, queue, swaps, chips, n_virt),
        out_shape=jax.ShapeDtypeStruct((pairs // n_virt, ab), f32),
        in_specs=[
            pl.BlockSpec(memory_space=pltpu.SMEM),
            pl.BlockSpec(memory_space=pltpu.VMEM),
            pl.BlockSpec(memory_space=pltpu.VMEM),
        ],
        out_specs=pl.BlockSpec(memory_space=pltpu.VMEM),
        scratch_shapes=[
            pltpu.VMEM((queue, ab, half), f32),
            pltpu.VMEM((swaps, pairs, half), f32),
            pltpu.VMEM((swaps, pairs, half), f32),
            pltpu.VMEM((swaps, rows, half), f32),
            pltpu.VMEM((swaps, rows, half), f32),
            pltpu.VMEM((pairs, ab), f32),
            pltpu.VMEM((n_virt - 1, pairs // n_virt, ab), f32),
            dma((2, swaps)),
            dma((2, swaps)),
            dma((queue, 2, chips - 1)),
            dma((queue, 2, chips - 1)),
            dma((queue, chips)),
            dma((queue, chips)),
            dma((n_virt - 1,)),
            dma((n_virt - 1,)),
        ],
        compiler_params=pltpu.CompilerParams(
            collective_id=call_id, has_side_effects=True, vmem_limit_bytes=58 * 1024 * 1024),
    )(counts, amplitudes, integrals)


def on_device(chips, n_virt, amplitudes, integrals, tile_flags, live_count, pair_occ, occ_energy, ab_energy):
    slots = amplitudes.shape[0]
    virt = lax.axis_index("virt")
    other = jnp.roll(live_count, -(n_virt // 2))
    mine, theirs = live_count[virt], other[virt]
    counts = jnp.stack([mine, jnp.minimum(2 * mine, mine + theirs), jnp.maximum(theirs - mine, 0)]).astype(jnp.int32)
    longest = jnp.max(live_count + other)
    sym_integrals = symmetric(integrals, tile_flags)
    least, most = slots + 1, 2 * slots
    ladder = lax.cond(
        longest <= least,
        functools.partial(contract, least, 1, chips, n_virt),
        functools.partial(contract, most, 2, chips, n_virt),
        counts, amplitudes, sym_integrals)
    occ_range = jnp.arange(occ_energy.shape[0], dtype=jnp.int32)
    first_energy = jnp.sum(
        jnp.where(pair_occ[:, 0:1] == occ_range[None, :], occ_energy[None, :], 0.0), axis=1
    )
    second_energy = jnp.sum(
        jnp.where(pair_occ[:, 1:2] == occ_range[None, :], occ_energy[None, :], 0.0), axis=1
    )
    denominator = ab_energy[None, :] - first_energy[:, None] - second_energy[:, None]
    return (ladder, ladder / denominator)


def solution(mesh):
    return jax.shard_map(
        functools.partial(on_device, mesh.shape["pair"] // CORES, mesh.shape["virt"]),
        mesh=mesh,
        in_specs=(
            P("virt", "pair", None),
            P("virt", "pair", None),
            P("virt"),
            P(),
            P(("pair", "virt"), None),
            P(),
            P(),
        ),
        out_specs=(P(("pair", "virt"), None), P(("pair", "virt"), None)),
        check_vma=False,
    )
```

```python
import functools

import jax
import jax.numpy as jnp
from jax import lax
from jax.experimental import pallas as pl
from jax.experimental.pallas import tpu as pltpu
from jax.sharding import PartitionSpec as P

TILE = 64
CORES = 2
DEPTH = 512
MESH = pl.DeviceIdType.MESH


def split(x):
    high = x.astype(jnp.bfloat16)
    return high, (x - high.astype(jnp.float32)).astype(jnp.bfloat16)


def product(a, b):
    a_high, a_low = split(a)
    b_high, b_low = split(b)

    def dot(x, y):
        return lax.dot_general(x, y, (((1,), (1,)), ((), ())), preferred_element_type=jnp.float32)

    return dot(a_high, b_high) + (dot(a_high, b_low) + dot(a_low, b_high))


def kernel(queue, swaps, inward, chips, n_virt, live_count, flags, a_ref, v_ref, out_ref, rows_all, a_out, a_in, v_out, v_in,
           v_sym, turned, a_end, acc, acc_end, acc_back, parts, xs, xr, zs, zr, cs, cr, es, er, rs, rr):
    pair = lax.axis_index("pair")
    virt = lax.axis_index("virt")
    z, core = pair // CORES, pair % CORES
    half = a_ref.shape[2] // 2
    slots = a_ref.shape[0]
    rows = v_ref.shape[1]
    pairs = a_ref.shape[1]
    out_rows = out_ref.shape[0]
    partner = lax.rem(virt + n_virt // 2, n_virt)
    live, theirs = live_count[virt], live_count[partner]
    keep = jnp.minimum(2 * live, live + theirs)
    taken = jnp.maximum(theirs - live, 0)
    is_end = (z == 0) | (z == chips - 1)
    by_end = (z == 1) | (z == chips - 2)
    toward = jnp.where(z < chips // 2, 1, -1)

    def chip_at(target):
        return (target * CORES + core, virt)

    twin = (z * CORES + 1 - core, virt)
    barrier = pltpu.get_barrier_semaphore()
    pl.semaphore_signal(barrier, inc=1, device_id=twin, device_id_type=MESH)
    for step in range(1, n_virt):
        pl.semaphore_signal(barrier, inc=1, device_id=(pair, lax.rem(virt + step, n_virt)), device_id_type=MESH)

    @pl.when(z > 0)
    def _():
        pl.semaphore_signal(barrier, inc=1, device_id=chip_at(z - 1), device_id_type=MESH)

    @pl.when(z < chips - 1)
    def _():
        pl.semaphore_signal(barrier, inc=1, device_id=chip_at(z + 1), device_id_type=MESH)

    greeted = n_virt + jnp.where(z > 0, 1, 0) + jnp.where(z < chips - 1, 1, 0)
    pl.semaphore_wait(barrier, greeted)

    def block(q, chip, core_at):
        start = pl.multiple_of((chip * CORES + core_at) * rows, 8)
        return rows_all.at[q, pl.ds(start, rows), :]

    def swap_a(j):
        return pltpu.make_async_remote_copy(
            src_ref=a_out.at[j], dst_ref=a_in.at[j], send_sem=xs.at[0, j], recv_sem=xr.at[0, j],
            device_id=(pair, partner), device_id_type=MESH)

    def swap_v(j):
        return pltpu.make_async_remote_copy(
            src_ref=v_out.at[j], dst_ref=v_in.at[j], send_sem=xs.at[1, j], recv_sem=xr.at[1, j],
            device_id=(pair, partner), device_id_type=MESH)

    def to_chip(q, way, hops):
        sign = 1 if way == 0 else -1
        ref = block(q, z - sign * hops, core)
        return pltpu.make_async_remote_copy(
            src_ref=ref, dst_ref=ref, send_sem=zs.at[q, way, hops], recv_sem=zr.at[q, way, hops],
            device_id=chip_at(z + sign), device_id_type=MESH)

    def from_chip(q, way, hops):
        sign = 1 if way == 0 else -1
        ref = block(q, z - sign * hops, core)
        return pltpu.make_async_remote_copy(
            src_ref=ref, dst_ref=ref, send_sem=zs.at[q, way, hops - 1], recv_sem=zr.at[q, way, hops - 1],
            device_id=chip_at(z - sign), device_id_type=MESH)

    def to_twin(q, chip):
        ref = block(q, chip, core)
        return pltpu.make_async_remote_copy(
            src_ref=ref, dst_ref=ref, send_sem=cs.at[q, chip], recv_sem=cr.at[q, chip],
            device_id=twin, device_id_type=MESH)

    def from_twin(q, chip):
        ref = block(q, chip, 1 - core)
        return pltpu.make_async_remote_copy(
            src_ref=ref, dst_ref=ref, send_sem=cs.at[q, chip], recv_sem=cr.at[q, chip],
            device_id=twin, device_id_type=MESH)

    def can_send(q, way, hops):
        last = 1 if q < inward else 0
        if way == 0:
            return (z - hops >= 0) & (z < chips - 1 - last)
        return (z + hops < chips) & (z > last)

    def can_get(q, way, hops):
        exists = z - hops >= 0 if way == 0 else z + hops < chips
        return exists & works(q)

    def works(q):
        return jnp.logical_not(is_end) if q < inward else z >= 0

    def end_a(q):
        return pltpu.make_async_remote_copy(
            src_ref=a_ref.at[q // 2, :, columns(q)], dst_ref=a_end.at[q], send_sem=es.at[q], recv_sem=er.at[q],
            device_id=chip_at(z + toward), device_id_type=MESH)

    def end_sums():
        return pltpu.make_async_remote_copy(
            src_ref=acc_end, dst_ref=acc_back, send_sem=es.at[inward], recv_sem=er.at[inward],
            device_id=chip_at(z - toward), device_id_type=MESH)

    def columns(unit):
        return slice((unit % 2) * half, (unit % 2 + 1) * half)

    def symmetrise(slot):
        lanes = 2 * TILE
        flag = flags[slot].astype(jnp.float32)

        @pl.loop(0, TILE // 2, unroll=4)
        def _(at):
            here = pl.ds(pl.multiple_of(at * lanes, lanes), lanes)
            turned[here, :] = v_ref[slot, :, here].T

        @pl.loop(0, TILE // 2, unroll=4)
        def _(at):
            here = pl.ds(pl.multiple_of(at * lanes, lanes), lanes)
            both = jnp.concatenate(
                [turned[pl.ds(2 * at, TILE, stride=TILE), :], turned[pl.ds(2 * at + 1, TILE, stride=TILE), :]], axis=0)
            v_sym[slot, :, here] = v_ref[slot, :, here] + flag * both.T

    def stage(q):
        own_unit = min(q, 2 * slots - 1)
        own = v_sym[own_unit // 2, :, columns(own_unit)]
        j = q - (queue - swaps)
        if j >= 0:
            swap_v(j).wait_recv()
            own = jnp.where(q >= queue - taken, v_in[j], own)
        start = pl.multiple_of(pair * rows, 8)
        rows_all[q, pl.ds(start, rows), :] = own
        for way in range(2):
            @pl.when(can_send(q, way, 0))
            def _():
                to_chip(q, way, 0).start()

        @pl.when(works(q))
        def _():
            to_twin(q, z).start()

    def relay(q):
        for hops in range(1, chips):
            for way in range(2):
                @pl.when(can_get(q, way, hops))
                def _():
                    from_chip(q, way, hops).wait_recv()
                    if hops < chips - 1:
                        @pl.when(can_send(q, way, hops))
                        def _():
                            to_chip(q, way, hops).start()
                    to_twin(q, z - hops if way == 0 else z + hops).start()

    def multiply(q):
        for chip in range(chips):
            from_twin(q, chip).wait_recv()
        own_unit = min(q, 2 * slots - 1)
        j = q - (queue - swaps)
        if j >= 0:
            swap_a(j).wait_recv()
        keep_own = q < keep
        base = (own_unit % 2) * half

        @pl.loop(0, half // DEPTH)
        def _(step):
            inner = pl.ds(pl.multiple_of(step * DEPTH, DEPTH), DEPTH)
            outer = pl.ds(pl.multiple_of(base + step * DEPTH, DEPTH), DEPTH)
            a = jnp.where(keep_own, a_ref[own_unit // 2, :, outer], 0.0)
            if j >= 0:
                a = jnp.where(q >= queue - taken, a_in[j, :, inner], a)
            acc[...] += product(a, rows_all[q, :, inner])

        if q < inward:
            @pl.when(by_end)
            def _():
                chip_in = end_a(q)
                chip_in.wait_recv()

                @pl.loop(0, half // DEPTH)
                def _(step):
                    inner = pl.ds(pl.multiple_of(step * DEPTH, DEPTH), DEPTH)
                    acc_end[...] += product(a_end[q, :, inner], rows_all[q, :, inner])

                if q == inward - 1:
                    end_sums().start()

    def source(j):
        return jnp.clip(live + (j - swaps) // 2, 0, slots - 1)

    for q in range(inward):
        @pl.when(is_end)
        def _():
            end_a(q).start()

    for j in range(swaps):
        a_out[j] = a_ref[source(j), :, columns(j - swaps)]
        swap_a(j).start()
    acc[...] = jnp.zeros_like(acc)
    acc_end[...] = jnp.zeros_like(acc_end)
    ahead = queue - swaps
    done = 0
    for q in range(min(2, ahead)):
        if q // 2 == done:
            symmetrise(done)
            done += 1
        stage(q)
    for slot in range(done, slots):
        symmetrise(slot)
    for j in range(swaps):
        v_out[j] = v_sym[source(j), :, columns(j - swaps)]
        swap_v(j).start()
    for q in range(2, ahead):
        stage(q)
    for q in range(queue):
        @pl.when(works(q))
        def _():
            relay(q)

        if q + ahead < queue:
            stage(q + ahead)

        @pl.when(works(q))
        def _():
            multiply(q)

    if inward:
        @pl.when(is_end)
        def _():
            end_sums().wait_recv()
            acc[...] += acc_back[...]

    def part(step):
        to = lax.rem(virt + step, n_virt)
        ref = acc.at[pl.ds(pl.multiple_of(to * out_rows, 8), out_rows), :]
        return pltpu.make_async_remote_copy(
            src_ref=ref, dst_ref=parts.at[step - 1], send_sem=rs.at[step - 1], recv_sem=rr.at[step - 1],
            device_id=(pair, to), device_id_type=MESH)

    for step in range(1, n_virt):
        part(step).start()
    total = acc[pl.ds(pl.multiple_of(virt * out_rows, 8), out_rows), :]
    for step in range(1, n_virt):
        part(step).wait_recv()
        total = total + parts[step - 1]
    out_ref[...] = total

    for step in range(1, n_virt):
        part(step).wait_send()
    for j in range(swaps):
        swap_a(j).wait_send()
        swap_v(j).wait_send()
    for q in range(inward):
        @pl.when(is_end)
        def _():
            end_a(q).wait_send()
    if inward:
        @pl.when(by_end)
        def _():
            end_sums().wait_send()
    for q in range(queue):
        for hops in range(chips - 1):
            for way in range(2):
                @pl.when(can_send(q, way, hops))
                def _():
                    to_chip(q, way, hops).wait_send()

        @pl.when(works(q))
        def _():
            for chip in range(chips):
                to_twin(q, chip).wait_send()


def contract(queue, call_id, chips, n_virt, live_count, tile_flags, amplitudes, integrals):
    slots, pairs, width = amplitudes.shape
    rows = integrals.shape[1]
    ab = rows * chips * CORES
    swaps, half = slots - 1, width // 2
    inward = 2 if chips > 3 else 0
    f32 = jnp.float32
    dma = pltpu.SemaphoreType.DMA
    return pl.pallas_call(
        functools.partial(kernel, queue, swaps, inward, chips, n_virt),
        out_shape=jax.ShapeDtypeStruct((pairs // n_virt, ab), f32),
        in_specs=[
            pl.BlockSpec(memory_space=pltpu.SMEM),
            pl.BlockSpec(memory_space=pltpu.SMEM),
            pl.BlockSpec(memory_space=pltpu.VMEM),
            pl.BlockSpec(memory_space=pltpu.VMEM),
        ],
        out_specs=pl.BlockSpec(memory_space=pltpu.VMEM),
        scratch_shapes=[
            pltpu.VMEM((queue, ab, half), f32),
            pltpu.VMEM((swaps, pairs, half), f32),
            pltpu.VMEM((swaps, pairs, half), f32),
            pltpu.VMEM((swaps, rows, half), f32),
            pltpu.VMEM((swaps, rows, half), f32),
            pltpu.VMEM((slots, rows, width), f32),
            pltpu.VMEM((width, rows), f32),
            pltpu.VMEM((max(inward, 1), pairs, half), f32),
            pltpu.VMEM((pairs, ab), f32),
            pltpu.VMEM((pairs, ab), f32),
            pltpu.VMEM((pairs, ab), f32),
            pltpu.VMEM((n_virt - 1, pairs // n_virt, ab), f32),
            dma((2, swaps)),
            dma((2, swaps)),
            dma((queue, 2, chips - 1)),
            dma((queue, 2, chips - 1)),
            dma((queue, chips)),
            dma((queue, chips)),
            dma((inward + 1,)),
            dma((inward + 1,)),
            dma((n_virt - 1,)),
            dma((n_virt - 1,)),
        ],
        compiler_params=pltpu.CompilerParams(
            collective_id=call_id, has_side_effects=True, vmem_limit_bytes=58 * 1024 * 1024),
    )(live_count, tile_flags, amplitudes, integrals)


def on_device(chips, n_virt, amplitudes, integrals, tile_flags, live_count, pair_occ, occ_energy, ab_energy):
    slots = amplitudes.shape[0]
    least, most = slots + 1, 2 * slots
    ladder = lax.cond(
        jnp.all(live_count + jnp.roll(live_count, n_virt // 2) <= least),
        functools.partial(contract, least, 1, chips, n_virt),
        functools.partial(contract, most, 2, chips, n_virt),
        live_count, tile_flags, amplitudes, integrals)
    occ_range = jnp.arange(occ_energy.shape[0], dtype=jnp.int32)
    first_energy = jnp.sum(
        jnp.where(pair_occ[:, 0:1] == occ_range[None, :], occ_energy[None, :], 0.0), axis=1
    )
    second_energy = jnp.sum(
        jnp.where(pair_occ[:, 1:2] == occ_range[None, :], occ_energy[None, :], 0.0), axis=1
    )
    denominator = ab_energy[None, :] - first_energy[:, None] - second_energy[:, None]
    return (ladder, ladder / denominator)


def solution(mesh):
    return jax.shard_map(
        functools.partial(on_device, mesh.shape["pair"] // CORES, mesh.shape["virt"]),
        mesh=mesh,
        in_specs=(
            P("virt", "pair", None),
            P("virt", "pair", None),
            P("virt"),
            P(),
            P(("pair", "virt"), None),
            P(),
            P(),
        ),
        out_specs=(P(("pair", "virt"), None), P(("pair", "virt"), None)),
        check_vma=False,
    )
```

```python
import functools

import jax
import jax.numpy as jnp
from jax import lax
from jax.experimental import pallas as pl
from jax.experimental.pallas import tpu as pltpu
from jax.sharding import PartitionSpec as P

TILE = 64
CORES = 2
DEPTH = 512
MESH = pl.DeviceIdType.MESH


def split(x):
    high = x.astype(jnp.bfloat16)
    return high, (x - high.astype(jnp.float32)).astype(jnp.bfloat16)


def product(a, b):
    a_high, a_low = split(a)
    b_high, b_low = split(b)

    def dot(x, y):
        return lax.dot_general(x, y, (((1,), (1,)), ((), ())), preferred_element_type=jnp.float32)

    return dot(a_high, b_high) + (dot(a_high, b_low) + dot(a_low, b_high))


def kernel(queue, swaps, inward, chips, n_virt, live_count, flags, a_ref, v_ref, out_ref, rows_all, a_out, a_in, v_out, v_in,
           v_sym, turned, a_end, acc, acc_end, acc_back, parts, xs, xr, zs, zr, cs, cr, es, er, rs, rr):
    pair = lax.axis_index("pair")
    virt = lax.axis_index("virt")
    z, core = pair // CORES, pair % CORES
    half = a_ref.shape[2] // 2
    slots = a_ref.shape[0]
    rows = v_ref.shape[1]
    pairs = a_ref.shape[1]
    out_rows = out_ref.shape[0]
    partner = lax.rem(virt + n_virt // 2, n_virt)
    live, theirs = live_count[virt], live_count[partner]
    keep = jnp.minimum(2 * live, live + theirs)
    taken = jnp.maximum(theirs - live, 0)
    is_end = (z == 0) | (z == chips - 1)
    by_end = (z == 1) | (z == chips - 2)
    toward = jnp.where(z < chips // 2, 1, -1)

    def chip_at(target):
        return (target * CORES + core, virt)

    twin = (z * CORES + 1 - core, virt)
    barrier = pltpu.get_barrier_semaphore()
    pl.semaphore_signal(barrier, inc=1, device_id=twin, device_id_type=MESH)
    for step in range(1, n_virt):
        pl.semaphore_signal(barrier, inc=1, device_id=(pair, lax.rem(virt + step, n_virt)), device_id_type=MESH)

    @pl.when(z > 0)
    def _():
        pl.semaphore_signal(barrier, inc=1, device_id=chip_at(z - 1), device_id_type=MESH)

    @pl.when(z < chips - 1)
    def _():
        pl.semaphore_signal(barrier, inc=1, device_id=chip_at(z + 1), device_id_type=MESH)

    greeted = n_virt + jnp.where(z > 0, 1, 0) + jnp.where(z < chips - 1, 1, 0)
    pl.semaphore_wait(barrier, greeted)

    def block(q, chip, core_at):
        start = pl.multiple_of((chip * CORES + core_at) * rows, 8)
        return rows_all.at[q, pl.ds(start, rows), :]

    def swap_a(j):
        return pltpu.make_async_remote_copy(
            src_ref=a_out.at[j], dst_ref=a_in.at[j], send_sem=xs.at[0, j], recv_sem=xr.at[0, j],
            device_id=(pair, partner), device_id_type=MESH)

    def swap_v(j):
        return pltpu.make_async_remote_copy(
            src_ref=v_out.at[j], dst_ref=v_in.at[j], send_sem=xs.at[1, j], recv_sem=xr.at[1, j],
            device_id=(pair, partner), device_id_type=MESH)

    def to_chip(q, way, hops):
        sign = 1 if way == 0 else -1
        ref = block(q, z - sign * hops, core)
        return pltpu.make_async_remote_copy(
            src_ref=ref, dst_ref=ref, send_sem=zs.at[q, way, hops], recv_sem=zr.at[q, way, hops],
            device_id=chip_at(z + sign), device_id_type=MESH)

    def from_chip(q, way, hops):
        sign = 1 if way == 0 else -1
        ref = block(q, z - sign * hops, core)
        return pltpu.make_async_remote_copy(
            src_ref=ref, dst_ref=ref, send_sem=zs.at[q, way, hops - 1], recv_sem=zr.at[q, way, hops - 1],
            device_id=chip_at(z - sign), device_id_type=MESH)

    def to_twin(q, chip):
        ref = block(q, chip, core)
        return pltpu.make_async_remote_copy(
            src_ref=ref, dst_ref=ref, send_sem=cs.at[q, chip], recv_sem=cr.at[q, chip],
            device_id=twin, device_id_type=MESH)

    def from_twin(q, chip):
        ref = block(q, chip, 1 - core)
        return pltpu.make_async_remote_copy(
            src_ref=ref, dst_ref=ref, send_sem=cs.at[q, chip], recv_sem=cr.at[q, chip],
            device_id=twin, device_id_type=MESH)

    def can_send(q, way, hops):
        last = 1 if q < inward else 0
        if way == 0:
            return (z - hops >= 0) & (z < chips - 1 - last)
        return (z + hops < chips) & (z > last)

    def can_get(q, way, hops):
        exists = z - hops >= 0 if way == 0 else z + hops < chips
        return exists & works(q)

    def works(q):
        return jnp.logical_not(is_end) if q < inward else z >= 0

    def end_a(q):
        return pltpu.make_async_remote_copy(
            src_ref=a_ref.at[q // 2, :, columns(q)], dst_ref=a_end.at[q], send_sem=es.at[q], recv_sem=er.at[q],
            device_id=chip_at(z + toward), device_id_type=MESH)

    def end_sums():
        return pltpu.make_async_remote_copy(
            src_ref=acc_end, dst_ref=acc_back, send_sem=es.at[inward], recv_sem=er.at[inward],
            device_id=chip_at(z - toward), device_id_type=MESH)

    def columns(unit):
        return slice((unit % 2) * half, (unit % 2 + 1) * half)

    def symmetrise(slot, halves):
        lanes = 2 * TILE
        flag = flags[slot].astype(jnp.float32)

        @pl.loop(0, TILE // 2, unroll=8)
        def _(at):
            here = pl.ds(pl.multiple_of(at * lanes, lanes), lanes)
            turned[here, :] = v_ref[slot, :, here].T

        for part_at, target in halves:
            first = part_at * (TILE // 4)

            @pl.loop(0, TILE // 4, unroll=8)
            def _(at):
                whole = pl.ds(pl.multiple_of((first + at) * lanes, lanes), lanes)
                here = pl.ds(pl.multiple_of(at * lanes, lanes), lanes)
                start = 2 * (first + at)
                both = jnp.concatenate(
                    [turned[pl.ds(start, TILE, stride=TILE), :], turned[pl.ds(start + 1, TILE, stride=TILE), :]], axis=0)
                target[:, here] = v_ref[slot, :, whole] + flag * both.T

    def symmetrise_own(slot):
        symmetrise(slot, [(at, v_sym.at[slot, :, pl.ds(at * half, half)]) for at in range(2)])

    def stage(q):
        own_unit = min(q, 2 * slots - 1)
        own = v_sym[own_unit // 2, :, columns(own_unit)]
        j = q - (queue - swaps)
        if j >= 0:
            swap_v(j).wait_recv()
            own = jnp.where(q >= queue - taken, v_in[j], own)
        start = pl.multiple_of(pair * rows, 8)
        rows_all[q, pl.ds(start, rows), :] = own
        for way in range(2):
            @pl.when(can_send(q, way, 0))
            def _():
                to_chip(q, way, 0).start()

        @pl.when(works(q))
        def _():
            to_twin(q, z).start()

    def relay(q, hops):
        for way in range(2):
            @pl.when(can_get(q, way, hops))
            def _():
                from_chip(q, way, hops).wait_recv()
                if hops < chips - 1:
                    @pl.when(can_send(q, way, hops))
                    def _():
                        to_chip(q, way, hops).start()
                to_twin(q, z - hops if way == 0 else z + hops).start()

    def multiply(q):
        for chip in range(chips):
            from_twin(q, chip).wait_recv()
        own_unit = min(q, 2 * slots - 1)
        j = q - (queue - swaps)
        if j >= 0:
            swap_a(j).wait_recv()
        keep_own = q < keep
        base = (own_unit % 2) * half

        @pl.loop(0, half // DEPTH)
        def _(step):
            inner = pl.ds(pl.multiple_of(step * DEPTH, DEPTH), DEPTH)
            outer = pl.ds(pl.multiple_of(base + step * DEPTH, DEPTH), DEPTH)
            a = jnp.where(keep_own, a_ref[own_unit // 2, :, outer], 0.0)
            if j >= 0:
                a = jnp.where(q >= queue - taken, a_in[j, :, inner], a)
            acc[...] += product(a, rows_all[q, :, inner])

    def multiply_end(q):
        end_a(q).wait_recv()

        @pl.loop(0, half // DEPTH)
        def _(step):
            inner = pl.ds(pl.multiple_of(step * DEPTH, DEPTH), DEPTH)
            acc_end[...] += product(a_end[q, :, inner], rows_all[q, :, inner])

        if q == inward - 1:
            end_sums().start()

    def source(j):
        return jnp.clip(live + (j - swaps) // 2, 0, slots - 1)

    acc[...] = jnp.zeros_like(acc)
    acc_end[...] = jnp.zeros_like(acc_end)
    ahead = queue - swaps
    leaving = {}
    for j in range(swaps):
        leaving.setdefault((j - swaps) // 2, []).append(j)
    for at, (back, places) in enumerate(sorted(leaving.items())):
        symmetrise(source(places[0]), [((j - swaps) % 2, v_out.at[j]) for j in places])
        for j in places:
            swap_v(j).start()
        if at == 0:
            symmetrise_own(0)
            for q in range(min(2, ahead)):
                stage(q)
    for j in range(swaps):
        a_out[j] = a_ref[source(j), :, columns(j - swaps)]
        swap_a(j).start()
    for slot in range(1, min(slots, (queue + 1) // 2)):
        symmetrise_own(slot)
    for q in range(inward):
        @pl.when(is_end)
        def _():
            end_a(q).start()

    for q in range(2, ahead):
        stage(q)
    for step in range(queue + chips - 2):
        if step + ahead < queue:
            stage(step + ahead)
        for hops in range(chips - 1, 0, -1):
            q = step - hops + 1
            if 0 <= q < queue:
                relay(q, hops)
        whole = step - chips + 2
        if 0 <= whole < ahead:
            @pl.when(works(whole))
            def _():
                multiply(whole)

    for q in range(ahead, queue):
        multiply(q)
        if q - ahead < inward:
            @pl.when(by_end)
            def _():
                multiply_end(q - ahead)

    if inward:
        @pl.when(is_end)
        def _():
            end_sums().wait_recv()
            acc[...] += acc_back[...]

    def part(step):
        to = lax.rem(virt + step, n_virt)
        ref = acc.at[pl.ds(pl.multiple_of(to * out_rows, 8), out_rows), :]
        return pltpu.make_async_remote_copy(
            src_ref=ref, dst_ref=parts.at[step - 1], send_sem=rs.at[step - 1], recv_sem=rr.at[step - 1],
            device_id=(pair, to), device_id_type=MESH)

    for step in range(1, n_virt):
        part(step).start()
    total = acc[pl.ds(pl.multiple_of(virt * out_rows, 8), out_rows), :]
    for step in range(1, n_virt):
        part(step).wait_recv()
        total = total + parts[step - 1]
    out_ref[...] = total

    for step in range(1, n_virt):
        part(step).wait_send()
    for j in range(swaps):
        swap_a(j).wait_send()
        swap_v(j).wait_send()
    for q in range(inward):
        @pl.when(is_end)
        def _():
            end_a(q).wait_send()
    if inward:
        @pl.when(by_end)
        def _():
            end_sums().wait_send()
    for q in range(queue):
        for hops in range(chips - 1):
            for way in range(2):
                @pl.when(can_send(q, way, hops))
                def _():
                    to_chip(q, way, hops).wait_send()

        @pl.when(works(q))
        def _():
            for chip in range(chips):
                to_twin(q, chip).wait_send()


def contract(queue, call_id, chips, n_virt, live_count, tile_flags, amplitudes, integrals):
    slots, pairs, width = amplitudes.shape
    rows = integrals.shape[1]
    ab = rows * chips * CORES
    swaps, half = slots - 1, width // 2
    inward = 1 if chips > 3 else 0
    f32 = jnp.float32
    dma = pltpu.SemaphoreType.DMA
    return pl.pallas_call(
        functools.partial(kernel, queue, swaps, inward, chips, n_virt),
        out_shape=jax.ShapeDtypeStruct((pairs // n_virt, ab), f32),
        in_specs=[
            pl.BlockSpec(memory_space=pltpu.SMEM),
            pl.BlockSpec(memory_space=pltpu.SMEM),
            pl.BlockSpec(memory_space=pltpu.VMEM),
            pl.BlockSpec(memory_space=pltpu.VMEM),
        ],
        out_specs=pl.BlockSpec(memory_space=pltpu.VMEM),
        scratch_shapes=[
            pltpu.VMEM((queue, ab, half), f32),
            pltpu.VMEM((swaps, pairs, half), f32),
            pltpu.VMEM((swaps, pairs, half), f32),
            pltpu.VMEM((swaps, rows, half), f32),
            pltpu.VMEM((swaps, rows, half), f32),
            pltpu.VMEM((slots, rows, width), f32),
            pltpu.VMEM((width, rows), f32),
            pltpu.VMEM((max(inward, 1), pairs, half), f32),
            pltpu.VMEM((pairs, ab), f32),
            pltpu.VMEM((pairs, ab), f32),
            pltpu.VMEM((pairs, ab), f32),
            pltpu.VMEM((n_virt - 1, pairs // n_virt, ab), f32),
            dma((2, swaps)),
            dma((2, swaps)),
            dma((queue, 2, chips - 1)),
            dma((queue, 2, chips - 1)),
            dma((queue, chips)),
            dma((queue, chips)),
            dma((inward + 1,)),
            dma((inward + 1,)),
            dma((n_virt - 1,)),
            dma((n_virt - 1,)),
        ],
        compiler_params=pltpu.CompilerParams(
            collective_id=call_id, has_side_effects=True, vmem_limit_bytes=58 * 1024 * 1024),
    )(live_count, tile_flags, amplitudes, integrals)


def on_device(chips, n_virt, amplitudes, integrals, tile_flags, live_count, pair_occ, occ_energy, ab_energy):
    slots = amplitudes.shape[0]
    lengths = [slots + 1, 2 * slots]
    both = live_count + jnp.roll(live_count, n_virt // 2)
    ladder = lax.switch(
        jnp.sum(jnp.any(both[:, None] > jnp.array(lengths[:-1])[None, :], axis=0).astype(jnp.int32)),
        [functools.partial(contract, length, at + 1, chips, n_virt) for at, length in enumerate(lengths)],
        live_count, tile_flags, amplitudes, integrals)
    occ_range = jnp.arange(occ_energy.shape[0], dtype=jnp.int32)
    first_energy = jnp.sum(
        jnp.where(pair_occ[:, 0:1] == occ_range[None, :], occ_energy[None, :], 0.0), axis=1
    )
    second_energy = jnp.sum(
        jnp.where(pair_occ[:, 1:2] == occ_range[None, :], occ_energy[None, :], 0.0), axis=1
    )
    denominator = ab_energy[None, :] - first_energy[:, None] - second_energy[:, None]
    return (ladder, ladder / denominator)


def solution(mesh):
    return jax.shard_map(
        functools.partial(on_device, mesh.shape["pair"] // CORES, mesh.shape["virt"]),
        mesh=mesh,
        in_specs=(
            P("virt", "pair", None),
            P("virt", "pair", None),
            P("virt"),
            P(),
            P(("pair", "virt"), None),
            P(),
            P(),
        ),
        out_specs=(P(("pair", "virt"), None), P(("pair", "virt"), None)),
        check_vma=False,
    )
```
